32 devices in a mesh: row: 4 (over y, core), col: 8 (over z, x).
Axes of the slice: x: 2, y: 2, z: 4, core: 2. Of those that a mesh axis runs over, the one named last changes fastest.
Arguments:
- upper_corner: bfloat16 [96, 96], P(None, 'row'), may hold values from -6 to 6
- right_corner: bfloat16 [96, 96], P(None, 'row'), may hold values from -6 to 6
- lower_corner: bfloat16 [96, 96], P(None, 'row'), may hold values from -6 to 6
- top_edge: bfloat16 [96, 96, 36], P('row', 'col'), may hold values from -0.625 to 0.625
- right_edge: bfloat16 [96, 96, 36], P('row', 'col'), may hold values from -0.625 to 0.625
- bottom_edge: bfloat16 [96, 96, 36], P('row', 'col'), may hold values from -0.625 to 0.625
- left_edge: bfloat16 [96, 96, 36], P('row', 'col'), may hold values from -0.625 to 0.625
- site_tensor: bfloat16 [1679616], replicated, may hold values from -0.15625 to 0.15625
- top_projector: bfloat16 [3456, 96], P('col'), may hold values from -0.109375 to 0.109375
- bottom_projector: bfloat16 [3456, 96], P('col'), may hold values from -0.109375 to 0.109375
Outputs:
- upper_half: bfloat16 [3456, 3456], P('row', 'col')
- left_half: bfloat16 [3456, 3456], P('col', 'row')
- corner_top: bfloat16 [96, 3456], P('col', 'row')
- corner_bottom: bfloat16 [96, 3456], P('col', 'row')
The draws below stay inside these ranges and needn't reach their ends.
All inputs are finite; a program needn't handle non-finite values.
Results may differ from the reference program's by a relative error of at most 0.0081.
Values may be sent and summed in bfloat16 or wider, within the bound.
A program may use at most 128 MiB of HBM per device.

```python
import jax
import jax.numpy as jnp

D = 6
CHI = 96
DD = 36
WIDE = 3456


def block_scale(stream_key, extent, cuts, least, largest):
    def one(axis_at, shards_of):
        heights = jax.random.uniform(jax.random.fold_in(jax.random.fold_in(stream_key, 6), axis_at), (shards_of,), jnp.float32, least / len(cuts), largest / len(cuts))
        return jnp.repeat(jnp.exp(heights), extent[axis_at] // shards_of).reshape((-1,) + (1,) * (len(extent) - axis_at - 1))

    gain = one(*cuts[0])
    for cut in cuts[1:]:
        gain = gain * one(*cut)
    return gain


def scatter_about(own_key, shape, spread, reach, split=(), kind=jnp.bfloat16):
    level = block_scale(own_key, shape, split, -0.22, 0.18) if split else 1.0
    values = jax.random.normal(own_key, shape, jnp.float32) * spread * level
    return jnp.minimum(jnp.maximum(values, -reach), reach).astype(kind)


def setup_inputs(seed: int = 0) -> dict:
    seeds = jax.random.split(jax.random.key(seed), 11)
    return {
        "upper_corner": scatter_about(seeds[0], (CHI, CHI), 1.0, 6.0, ((1, 4),)),
        "right_corner": scatter_about(seeds[1], (CHI, CHI), 1.0, 6.0, ((1, 4),)),
        "lower_corner": scatter_about(seeds[2], (CHI, CHI), 1.0, 6.0, ((1, 4),)),
        "top_edge": scatter_about(seeds[3], (CHI, CHI, DD), CHI ** -0.5, 0.625, ((0, 4), (1, 8))),
        "right_edge": scatter_about(seeds[4], (CHI, CHI, DD), CHI ** -0.5, 0.625, ((0, 4), (1, 8))),
        "bottom_edge": scatter_about(seeds[5], (CHI, CHI, DD), CHI ** -0.5, 0.625, ((0, 4), (1, 8))),
        "left_edge": scatter_about(seeds[6], (CHI, CHI, DD), CHI ** -0.5, 0.625, ((0, 4), (1, 8))),
        "site_tensor": scatter_about(seeds[7], (D ** 8,), (D ** 4) ** -0.5, 0.15625),
        "top_projector": scatter_about(seeds[8], (WIDE, CHI), WIDE ** -0.5, 0.109375, ((0, 8),)),
        "bottom_projector": scatter_about(seeds[9], (WIDE, CHI), WIDE ** -0.5, 0.109375, ((0, 8),)),
    }


def absorb(corner, edge):
    return jnp.einsum("cd,dbv->cbv", corner.astype(jnp.float32), edge.astype(jnp.float32)).astype(jnp.bfloat16)


def contract(form, first, second):
    return jnp.einsum(form, first.astype(jnp.float32), second.astype(jnp.float32)).astype(jnp.bfloat16)


def reference(upper_corner, right_corner, lower_corner, top_edge, right_edge, bottom_edge, left_edge, site_tensor, top_projector, bottom_projector):
    composite = CHI * D * D
    factor = composite ** -0.5
    double = D * D
    site = site_tensor.reshape(double, double, double, double)
    absorbed_top = absorb(upper_corner, top_edge)
    absorbed_right = absorb(right_corner, right_edge)
    absorbed_bottom = absorb(lower_corner, bottom_edge)
    partial_top = contract("acu,cbv->aubv", left_edge, absorbed_top)
    partial_right = contract("bdv,dgw->bvgw", top_edge, absorbed_right)
    partial_bottom = contract("cau,cbv->aubv", left_edge, absorbed_bottom)
    enlarged_top = contract("aubv,vust->asbt", partial_top, site).reshape(composite, composite)
    enlarged_right = contract("bvgw,vtsw->btgs", partial_right, site).reshape(composite, composite)
    enlarged_bottom = contract("aubv,suvt->asbt", partial_bottom, site).reshape(composite, composite)
    upper_half = (jnp.dot(enlarged_top, enlarged_right, preferred_element_type=jnp.float32) * factor).astype(jnp.bfloat16)
    left_half = (jnp.dot(enlarged_top.T, enlarged_bottom, preferred_element_type=jnp.float32) * factor).astype(jnp.bfloat16)
    corner_top = jnp.dot(top_projector.T, enlarged_top.T, preferred_element_type=jnp.float32).astype(jnp.bfloat16)
    corner_bottom = jnp.dot(bottom_projector.T, enlarged_bottom.T, preferred_element_type=jnp.float32).astype(jnp.bfloat16)
    return upper_half, left_half, corner_top, corner_bottom
```

```python
import functools

import jax
import jax.numpy as jnp
from jax import lax
from jax.experimental import pallas as pl
from jax.experimental.pallas import tpu as pltpu
from jax.sharding import PartitionSpec as P

ROWS = 16


def exchange(source, target, outer, inner, height, width):
    @pl.loop(0, height // ROWS)
    def _(tile):
        start = pl.multiple_of(tile * ROWS, ROWS)
        for i in range(inner):
            target[pl.ds(start + i * height, ROWS), :] = jnp.concatenate(
                [
                    source[pl.ds(start + o * height, ROWS), i * width : (i + 1) * width]
                    for o in range(outer)
                ],
                axis=1,
            )


def enlarge_kernel(own, height, double, flipped, first, site, panel, paired, product):
    exchange(first, paired, double, own, height, double)
    chunk = height * (4 if own % 4 == 0 else 2 if own % 2 == 0 else 1)
    form = (((1,), (1 if flipped else 0,)), ((), ()))

    @pl.loop(0, own * height // chunk)
    def _(at):
        rows = pl.ds(pl.multiple_of(at * chunk, chunk), chunk)
        product[rows, :] = lax.dot_general(
            paired[rows, :], site[...], form, preferred_element_type=jnp.float32
        ).astype(product.dtype)

    exchange(product, panel, own, double, height, double)


def enlarge(first, site, own, height, double, flipped):
    square = double * double
    return pl.pallas_call(
        functools.partial(enlarge_kernel, own, height, double, flipped),
        out_shape=jax.ShapeDtypeStruct((double * height, own * double), jnp.bfloat16),
        in_specs=[pl.BlockSpec(memory_space=pltpu.VMEM)] * 2,
        out_specs=pl.BlockSpec(memory_space=pltpu.VMEM),
        scratch_shapes=[pltpu.VMEM((own * height, square), jnp.bfloat16)] * 2,
        compiler_params=pltpu.CompilerParams(vmem_limit_bytes=50 * 1024 * 1024),
        cost_estimate=pl.CostEstimate(
            flops=2 * own * height * square * square,
            bytes_accessed=2 * square * square + 4 * own * height * square,
            transcendentals=0,
        ),
    )(first, site)


def dot(first, second):
    return jnp.dot(first, second, preferred_element_type=jnp.float32).astype(jnp.bfloat16)


def shards(
    upper_corner,
    right_corner,
    lower_corner,
    top_edge,
    right_edge,
    bottom_edge,
    left_edge,
    site_tensor,
    top_projector,
    bottom_projector,
):
    rows, cols = lax.axis_size("row"), lax.axis_size("col")
    row, col = lax.axis_index("row"), lax.axis_index("col")
    tall, wide, double = top_edge.shape
    chi = upper_corner.shape[0]
    square = double * double
    factor = (chi * double) ** (-0.5)

    slim = chi // cols
    corners = jnp.stack([upper_corner, right_corner, lower_corner])
    corners = lax.dynamic_slice_in_dim(corners, col * slim, slim, 1)
    packed = jnp.concatenate(
        [
            top_edge.reshape(-1),
            left_edge.reshape(-1),
            bottom_edge.reshape(-1),
            corners.reshape(-1),
        ]
    )
    whole = lax.all_gather(packed, ("row", "col"), axis=0)
    right_cols = lax.all_gather(right_edge, "row", axis=0, tiled=True)
    projectors = lax.all_gather(
        jnp.concatenate([top_projector, bottom_projector], axis=1), "col", axis=0, tiled=True
    )

    block = tall * wide * double

    def unpack(at):
        part = whole[:, at * block : (at + 1) * block]
        part = part.reshape(rows, cols, tall, wide, double)
        return part.transpose(0, 2, 1, 3, 4).reshape(chi, chi, double)

    top, left, bottom = unpack(0), unpack(1), unpack(2)
    corners = whole[:, 3 * block :].reshape(rows, cols, 3, slim, tall)
    corners = corners.transpose(2, 1, 3, 0, 4).reshape(3, chi, chi)
    upper, right, lower = corners[0], corners[1], corners[2]

    natural = site_tensor.reshape(square, square)
    legs = natural.reshape(double, double, square)
    site_col = legs.transpose(1, 0, 2).reshape(square, square)
    site_row = natural.T.reshape(double, double, square).transpose(1, 0, 2).reshape(square, square)
    site_side = natural.reshape((double,) * 4).transpose(1, 2, 0, 3).reshape(square, square)

    def flat(edge):
        return edge.reshape(edge.shape[0], edge.shape[1] * edge.shape[2])

    left_rows = lax.dynamic_slice_in_dim(left, row * tall, tall, 0)
    top_cols = lax.dynamic_slice_in_dim(top, col * wide, wide, 1)
    bottom_cols = lax.dynamic_slice_in_dim(bottom, row * tall, tall, 1)

    top_first = top.transpose(2, 1, 0).reshape(double * chi, chi)
    top_second = top.transpose(2, 0, 1).reshape(double * chi, chi)
    left_first = left.transpose(2, 1, 0).reshape(double * chi, chi)
    left_second = left.transpose(2, 0, 1).reshape(double * chi, chi)

    absorbed_bottom = dot(lower, flat(bottom_cols))
    absorbed_top = dot(upper, flat(top_cols))
    absorbed_right = dot(right, flat(right_cols))
    absorbed_turned = dot(top_first, upper.T)

    bottom_panel = enlarge(
        dot(left_first, absorbed_bottom), site_side, tall, chi, double, False
    )
    top_panel = enlarge(
        dot(absorbed_turned, flat(left_rows.transpose(1, 0, 2))), site_row, tall, chi, double, True
    )
    top_side = enlarge(dot(left_second, absorbed_top), site_col, wide, chi, double, False)
    right_panel = enlarge(dot(top_second, absorbed_right), site_side, wide, chi, double, True)

    projectors = projectors.reshape(chi, double, 2, chi)
    projectors = lax.dynamic_slice_in_dim(projectors, col * slim, slim, 3)
    top_share = projectors[:, :, 0].transpose(2, 1, 0).reshape(slim, double * chi)
    bottom_share = lax.dynamic_slice_in_dim(projectors[:, :, 1], row * tall, tall, 0)
    bottom_share = bottom_share.transpose(2, 0, 1).reshape(slim, tall * double)

    bottom_term = lax.dot_general(
        bottom_share, bottom_panel, (((1,), (1,)), ((), ())), preferred_element_type=jnp.float32
    )
    bottom_term = bottom_term.reshape(slim, double, chi).transpose(0, 2, 1)
    bottom_term = bottom_term.reshape(slim, chi * double)
    corner_bottom = lax.psum_scatter(bottom_term, "row", scatter_dimension=1, tiled=True)
    corner_bottom = corner_bottom.astype(jnp.bfloat16)
    corner_top = dot(top_share, top_panel)

    def joined(first, second):
        total = lax.dot_general(
            first, second, (((0,), (0,)), ((), ())), preferred_element_type=jnp.float32
        )
        return (total * factor).astype(jnp.bfloat16)

    left_half = joined(top_side, bottom_panel)
    upper_half = joined(top_panel, right_panel)
    return (upper_half, left_half, corner_top, corner_bottom)


def solution(mesh):
    placed = (
        P(None, "row"),
        P(None, "row"),
        P(None, "row"),
        P("row", "col", None),
        P("row", "col", None),
        P("row", "col", None),
        P("row", "col", None),
        P(),
        P("col", None),
        P("col", None),
    )
    return jax.shard_map(
        shards,
        mesh=mesh,
        in_specs=placed,
        out_specs=(P("row", "col"), P("col", "row"), P("col", "row"), P("col", "row")),
        check_vma=False,
    )
```

```python
import functools

import jax
import jax.numpy as jnp
from jax import lax
from jax.experimental import pallas as pl
from jax.experimental.pallas import tpu as pltpu
from jax.sharding import PartitionSpec as P

ROWS = 16


def exchange(source, target, outer, inner, height, width):
    @pl.loop(0, height // ROWS)
    def _(tile):
        start = pl.multiple_of(tile * ROWS, ROWS)
        for i in range(inner):
            target[pl.ds(start + i * height, ROWS), :] = jnp.concatenate(
                [
                    source[pl.ds(start + o * height, ROWS), i * width : (i + 1) * width]
                    for o in range(outer)
                ],
                axis=1,
            )


def enlarge_kernel(own, height, double, flipped, left, right, site, panel, paired, product):
    strip = height * (4 if double % 4 == 0 else 1)

    @pl.loop(0, double * height // strip)
    def _(at):
        rows = pl.ds(pl.multiple_of(at * strip, strip), strip)
        panel[rows, :] = jnp.dot(
            left[rows, :], right[...], preferred_element_type=jnp.float32
        ).astype(panel.dtype)

    exchange(panel, paired, double, own, height, double)
    chunk = height * (4 if own % 4 == 0 else 2 if own % 2 == 0 else 1)
    form = (((1,), (1 if flipped else 0,)), ((), ()))

    @pl.loop(0, own * height // chunk)
    def _(at):
        rows = pl.ds(pl.multiple_of(at * chunk, chunk), chunk)
        product[rows, :] = lax.dot_general(
            paired[rows, :], site[...], form, preferred_element_type=jnp.float32
        ).astype(product.dtype)

    exchange(product, panel, own, double, height, double)


def enlarge(left, right, site, own, height, double, flipped):
    square = double * double
    return pl.pallas_call(
        functools.partial(enlarge_kernel, own, height, double, flipped),
        out_shape=jax.ShapeDtypeStruct((double * height, own * double), jnp.bfloat16),
        in_specs=[pl.BlockSpec(memory_space=pltpu.VMEM)] * 3,
        out_specs=pl.BlockSpec(memory_space=pltpu.VMEM),
        scratch_shapes=[pltpu.VMEM((own * height, square), jnp.bfloat16)] * 2,
        compiler_params=pltpu.CompilerParams(vmem_limit_bytes=50 * 1024 * 1024),
        cost_estimate=pl.CostEstimate(
            flops=2 * own * height * square * square,
            bytes_accessed=2 * square * square + 4 * own * height * square,
            transcendentals=0,
        ),
    )(left, right, site)


def dot(first, second):
    return jnp.dot(first, second, preferred_element_type=jnp.float32).astype(jnp.bfloat16)


def shards(
    upper_corner,
    right_corner,
    lower_corner,
    top_edge,
    right_edge,
    bottom_edge,
    left_edge,
    site_tensor,
    top_projector,
    bottom_projector,
):
    rows, cols = lax.axis_size("row"), lax.axis_size("col")
    row, col = lax.axis_index("row"), lax.axis_index("col")
    tall, wide, double = top_edge.shape
    chi = upper_corner.shape[0]
    square = double * double
    factor = (chi * double) ** (-0.5)

    slim = chi // cols
    corners = jnp.stack([upper_corner, right_corner, lower_corner])
    corners = lax.dynamic_slice_in_dim(corners, col * slim, slim, 1)
    packed = jnp.concatenate(
        [
            top_edge.reshape(-1),
            left_edge.reshape(-1),
            bottom_edge.reshape(-1),
            corners.reshape(-1),
        ]
    )
    whole = lax.all_gather(packed[None], "col", axis=0, tiled=True)
    whole = lax.all_gather(whole, "row", axis=0, tiled=True)
    right_cols = lax.all_gather(right_edge, "row", axis=0, tiled=True)
    projectors = lax.all_gather(
        jnp.concatenate([top_projector, bottom_projector], axis=1), "col", axis=0, tiled=True
    )

    block = tall * wide * double

    def unpack(at):
        part = whole[:, at * block : (at + 1) * block]
        part = part.reshape(rows, cols, tall, wide, double)
        return part.transpose(0, 2, 1, 3, 4).reshape(chi, chi, double)

    top, left, bottom = unpack(0), unpack(1), unpack(2)
    corners = whole[:, 3 * block :].reshape(rows, cols, 3, slim, tall)
    corners = corners.transpose(2, 1, 3, 0, 4).reshape(3, chi, chi)
    upper, right, lower = corners[0], corners[1], corners[2]

    natural = site_tensor.reshape(square, square)
    legs = natural.reshape(double, double, square)
    site_col = legs.transpose(1, 0, 2).reshape(square, square)
    site_row = natural.T.reshape(double, double, square).transpose(1, 0, 2).reshape(square, square)
    site_side = natural.reshape((double,) * 4).transpose(1, 2, 0, 3).reshape(square, square)

    def flat(edge):
        return edge.reshape(edge.shape[0], edge.shape[1] * edge.shape[2])

    left_rows = lax.dynamic_slice_in_dim(left, row * tall, tall, 0)
    top_cols = lax.dynamic_slice_in_dim(top, col * wide, wide, 1)
    bottom_cols = lax.dynamic_slice_in_dim(bottom, row * tall, tall, 1)

    top_first = top.transpose(2, 1, 0).reshape(double * chi, chi)
    top_second = top.transpose(2, 0, 1).reshape(double * chi, chi)
    left_first = left.transpose(2, 1, 0).reshape(double * chi, chi)
    left_second = left.transpose(2, 0, 1).reshape(double * chi, chi)

    absorbed_bottom = dot(lower, flat(bottom_cols))
    absorbed_top = dot(upper, flat(top_cols))
    absorbed_right = dot(right, flat(right_cols))
    absorbed_turned = dot(top_first, upper.T)

    bottom_panel = enlarge(
        left_first, absorbed_bottom, site_side, tall, chi, double, False
    )
    projectors = projectors.reshape(chi, double, 2, chi)
    projectors = lax.dynamic_slice_in_dim(projectors, col * slim, slim, 3)
    top_share = projectors[:, :, 0].transpose(2, 1, 0).reshape(slim, double * chi)
    bottom_share = lax.dynamic_slice_in_dim(projectors[:, :, 1], row * tall, tall, 0)
    bottom_share = bottom_share.transpose(2, 0, 1).reshape(slim, tall * double)

    bottom_term = lax.dot_general(
        bottom_share, bottom_panel, (((1,), (1,)), ((), ())), preferred_element_type=jnp.float32
    )
    bottom_term = bottom_term.reshape(slim, double, chi).transpose(0, 2, 1)
    bottom_term = bottom_term.reshape(slim, chi * double)
    absorbed_turned, bottom_term = lax.optimization_barrier((absorbed_turned, bottom_term))
    corner_bottom = lax.psum_scatter(bottom_term, "row", scatter_dimension=1, tiled=True)
    corner_bottom = corner_bottom.astype(jnp.bfloat16)
    top_panel = enlarge(
        absorbed_turned, flat(left_rows.transpose(1, 0, 2)), site_row, tall, chi, double, True
    )
    top_side = enlarge(left_second, absorbed_top, site_col, wide, chi, double, False)
    right_panel = enlarge(top_second, absorbed_right, site_side, wide, chi, double, True)

    corner_top = dot(top_share, top_panel)

    def joined(first, second):
        total = lax.dot_general(
            first, second, (((0,), (0,)), ((), ())), preferred_element_type=jnp.float32
        )
        return (total * factor).astype(jnp.bfloat16)

    left_half = joined(top_side, bottom_panel)
    upper_half = joined(top_panel, right_panel)
    return (upper_half, left_half, corner_top, corner_bottom)


def solution(mesh):
    placed = (
        P(None, "row"),
        P(None, "row"),
        P(None, "row"),
        P("row", "col", None),
        P("row", "col", None),
        P("row", "col", None),
        P("row", "col", None),
        P(),
        P("col", None),
        P("col", None),
    )
    return jax.shard_map(
        shards,
        mesh=mesh,
        in_specs=placed,
        out_specs=(P("row", "col"), P("col", "row"), P("col", "row"), P("col", "row")),
        check_vma=False,
    )
```

```python
import functools

import jax
import jax.numpy as jnp
from jax import lax
from jax.experimental import pallas as pl
from jax.experimental.pallas import tpu as pltpu
from jax.sharding import PartitionSpec as P

ROWS = 16


def exchange(source, target, outer, inner, height, width):
    @pl.loop(0, height // ROWS)
    def _(tile):
        start = pl.multiple_of(tile * ROWS, ROWS)
        for i in range(inner):
            target[pl.ds(start + i * height, ROWS), :] = jnp.concatenate(
                [
                    source[pl.ds(start + o * height, ROWS), i * width : (i + 1) * width]
                    for o in range(outer)
                ],
                axis=1,
            )


def enlarge_kernel(own, height, double, flipped, left, right, site, panel, paired, product):
    strip = height * (4 if double % 4 == 0 else 1)

    @pl.loop(0, double * height // strip)
    def _(at):
        rows = pl.ds(pl.multiple_of(at * strip, strip), strip)
        panel[rows, :] = jnp.dot(
            left[rows, :], right[...], preferred_element_type=jnp.float32
        ).astype(panel.dtype)

    exchange(panel, paired, double, own, height, double)
    chunk = height * (4 if own % 4 == 0 else 2 if own % 2 == 0 else 1)
    form = (((1,), (1 if flipped else 0,)), ((), ()))

    @pl.loop(0, own * height // chunk)
    def _(at):
        rows = pl.ds(pl.multiple_of(at * chunk, chunk), chunk)
        product[rows, :] = lax.dot_general(
            paired[rows, :], site[...], form, preferred_element_type=jnp.float32
        ).astype(product.dtype)

    exchange(product, panel, own, double, height, double)


def enlarge(left, right, site, own, height, double, flipped):
    square = double * double
    return pl.pallas_call(
        functools.partial(enlarge_kernel, own, height, double, flipped),
        out_shape=jax.ShapeDtypeStruct((double * height, own * double), jnp.bfloat16),
        in_specs=[pl.BlockSpec(memory_space=pltpu.VMEM)] * 3,
        out_specs=pl.BlockSpec(memory_space=pltpu.VMEM),
        scratch_shapes=[pltpu.VMEM((own * height, square), jnp.bfloat16)] * 2,
        compiler_params=pltpu.CompilerParams(vmem_limit_bytes=50 * 1024 * 1024),
        cost_estimate=pl.CostEstimate(
            flops=2 * own * height * square * square,
            bytes_accessed=2 * square * square + 4 * own * height * square,
            transcendentals=0,
        ),
    )(left, right, site)


def dot(first, second):
    return jnp.dot(first, second, preferred_element_type=jnp.float32).astype(jnp.bfloat16)


def shards(
    upper_corner,
    right_corner,
    lower_corner,
    top_edge,
    right_edge,
    bottom_edge,
    left_edge,
    site_tensor,
    top_projector,
    bottom_projector,
):
    rows, cols = lax.axis_size("row"), lax.axis_size("col")
    row, col = lax.axis_index("row"), lax.axis_index("col")
    tall, wide, double = top_edge.shape
    chi = upper_corner.shape[0]
    square = double * double
    factor = (chi * double) ** (-0.5)

    slim = chi // cols
    corners = jnp.stack([upper_corner, right_corner, lower_corner])
    corners = lax.dynamic_slice_in_dim(corners, col * slim, slim, 1)
    packed = jnp.concatenate(
        [
            top_edge.reshape(-1),
            left_edge.reshape(-1),
            bottom_edge.reshape(-1),
            corners.reshape(-1),
        ]
    )
    whole = lax.all_gather(packed[None], "col", axis=0, tiled=True)
    natural = site_tensor.reshape(square, square)
    site_side = natural.reshape((double,) * 4).transpose(1, 2, 0, 3).reshape(square, square)
    whole, site_side = lax.optimization_barrier((whole, site_side))
    whole = lax.all_gather(whole, "row", axis=0, tiled=True)
    right_cols = lax.all_gather(right_edge, "row", axis=0, tiled=True)
    projectors = lax.all_gather(
        jnp.concatenate([top_projector, bottom_projector], axis=1), "col", axis=0, tiled=True
    )

    block = tall * wide * double

    def unpack(at):
        part = whole[:, at * block : (at + 1) * block]
        part = part.reshape(rows, cols, tall, wide, double)
        return part.transpose(0, 2, 1, 3, 4).reshape(chi, chi, double)

    top, left, bottom = unpack(0), unpack(1), unpack(2)
    corners = whole[:, 3 * block :].reshape(rows, cols, 3, slim, tall)
    corners = corners.transpose(2, 1, 3, 0, 4).reshape(3, chi, chi)
    upper, right, lower = corners[0], corners[1], corners[2]

    legs = natural.reshape(double, double, square)
    site_col = legs.transpose(1, 0, 2).reshape(square, square)
    site_row = natural.T.reshape(double, double, square).transpose(1, 0, 2).reshape(square, square)

    def flat(edge):
        return edge.reshape(edge.shape[0], edge.shape[1] * edge.shape[2])

    left_rows = lax.dynamic_slice_in_dim(left, row * tall, tall, 0)
    top_cols = lax.dynamic_slice_in_dim(top, col * wide, wide, 1)
    bottom_cols = lax.dynamic_slice_in_dim(bottom, row * tall, tall, 1)

    top_first = top.transpose(2, 1, 0).reshape(double * chi, chi)
    top_second = top.transpose(2, 0, 1).reshape(double * chi, chi)
    left_first = left.transpose(2, 1, 0).reshape(double * chi, chi)
    left_second = left.transpose(2, 0, 1).reshape(double * chi, chi)

    absorbed_bottom = dot(lower, flat(bottom_cols))
    absorbed_top = dot(upper, flat(top_cols))
    absorbed_right = dot(right, flat(right_cols))
    absorbed_turned = dot(top_first, upper.T)

    bottom_panel = enlarge(
        left_first, absorbed_bottom, site_side, tall, chi, double, False
    )
    projectors = projectors.reshape(chi, double, 2, chi)
    projectors = lax.dynamic_slice_in_dim(projectors, col * slim, slim, 3)
    top_share = projectors[:, :, 0].transpose(2, 1, 0).reshape(slim, double * chi)
    bottom_share = lax.dynamic_slice_in_dim(projectors[:, :, 1], row * tall, tall, 0)
    bottom_share = bottom_share.transpose(2, 0, 1).reshape(slim, tall * double)

    bottom_term = lax.dot_general(
        bottom_share, bottom_panel, (((1,), (1,)), ((), ())), preferred_element_type=jnp.float32
    )
    bottom_term = bottom_term.reshape(slim, double, chi).transpose(0, 2, 1)
    bottom_term = bottom_term.reshape(slim, chi * double)
    absorbed_turned, bottom_term = lax.optimization_barrier((absorbed_turned, bottom_term))
    corner_bottom = lax.psum_scatter(bottom_term, "row", scatter_dimension=1, tiled=True)
    corner_bottom = corner_bottom.astype(jnp.bfloat16)
    top_panel = enlarge(
        absorbed_turned, flat(left_rows.transpose(1, 0, 2)), site_row, tall, chi, double, True
    )
    top_side = enlarge(left_second, absorbed_top, site_col, wide, chi, double, False)
    right_panel = enlarge(top_second, absorbed_right, site_side, wide, chi, double, True)

    corner_top = dot(top_share, top_panel)

    def joined(first, second):
        total = lax.dot_general(
            first, second, (((0,), (0,)), ((), ())), preferred_element_type=jnp.float32
        )
        return (total * factor).astype(jnp.bfloat16)

    left_half = joined(top_side, bottom_panel)
    upper_half = joined(top_panel, right_panel)
    return (upper_half, left_half, corner_top, corner_bottom)


def solution(mesh):
    placed = (
        P(None, "row"),
        P(None, "row"),
        P(None, "row"),
        P("row", "col", None),
        P("row", "col", None),
        P("row", "col", None),
        P("row", "col", None),
        P(),
        P("col", None),
        P("col", None),
    )
    return jax.shard_map(
        shards,
        mesh=mesh,
        in_specs=placed,
        out_specs=(P("row", "col"), P("col", "row"), P("col", "row"), P("col", "row")),
        check_vma=False,
    )
```
